32 devices in a mesh: groups: 2 (over y), rows: 8 (over z, x), tp: 2 (over core).
Axes of the slice: x: 2, y: 2, z: 4, core: 2. Of those that a mesh axis runs over, the one named last changes fastest.
Arguments:
- activations: bfloat16 [2048, 4096], P(('groups', 'rows'), 'tp'), parts along dimension 0, may hold values from -6 to 6
- cotangent: bfloat16 [2048, 16384], P(('groups', 'rows'), 'tp'), parts along dimension 0, may hold values from -0.039794922 to 0.039794922
- adapter_down_factors: bfloat16 [16, 4096, 16], P('rows', 'tp'), may hold values from -1.796875 to 1.796875
- adapter_up_factors: bfloat16 [16, 16384, 16], P('rows', 'tp'), may hold values from -0.8984375 to 0.8984375
- adapter_slot: int32 [16], replicated, may hold values from 0 to 15, each once
- adapter_of_block: int32 [16], P('groups'), parts along dimension 0, may hold values from 0 to 15, as said below
- counts: int32 [32], P('groups'), parts along dimension 0, may hold values from 0 to 512, as said below
Outputs:
- input_grad: bfloat16 [2048, 4096], P(('groups', 'rows'), 'tp'), parts along dimension 0
- grad_down: bfloat16 [32, 4096, 16], P(('groups', 'rows'), 'tp'), parts along dimension 0
- grad_up: bfloat16 [32, 16384, 16], P(('groups', 'rows'), 'tp'), parts along dimension 0
The draws below stay inside these ranges and needn't reach their ends.
There are 2 independent parts, one for each index of `groups`. The reference program is written for one: setup_inputs(seed, part) draws one part's arguments, and reference() takes and returns one part's arrays. A program takes and returns all parts, laid end to end along the dimension named above; an argument that names none is the same for every part. Nothing has to cross between parts.
Inputs may be any that keep to these rules, and one draw needn't show every extreme that they name: `adapter_of_block`: an adapter number; an adapter may own several blocks, and most own none. counts[a] is 0 when no block names adapter a; else it lies between 128 * (n - 1) + 1 and 128 * n, n being the number of blocks that name a; one adapter has exactly 128 * (8 // 2) rows. `adapter_slot`: each slot once.
All inputs are finite; a program needn't handle non-finite values.
Results may differ from the reference program's by a relative error of at most 0.0051.
Values may be sent and summed in bfloat16 or wider, within the bound.
A program may use at most 64 MiB of HBM per device.

```python
import jax
import jax.numpy as jnp

INPUT_FEATURES = 4096
HIDDEN_WIDTH = 16384
ADAPTER_RANK = 16
BLK = 128
ADAPTER_TOTAL = 16
NBLOCKS = 8
TOKENS = 1024


def adapter_plan(key):
    first, second, third, order, spots = jax.random.split(key, 5)
    shape = (NBLOCKS,)
    others = ADAPTER_TOTAL - 1
    lowest = jnp.minimum(jax.random.randint(first, shape, 0, others), jax.random.randint(second, shape, 0, others))
    lowest = jnp.minimum(lowest, jax.random.randint(third, shape, 0, others))
    relabel = jax.random.permutation(order, others).astype(jnp.int32)
    chosen = relabel[lowest].astype(jnp.int32)
    placing = jax.random.permutation(spots, NBLOCKS).astype(jnp.int32)
    heavy = placing < NBLOCKS // 2
    chosen = jnp.where(heavy, ADAPTER_TOTAL - 1, chosen).astype(jnp.int32)
    labels = jnp.arange(ADAPTER_TOTAL, dtype=jnp.int32)
    blocks = jnp.sum((chosen[:, None] == labels[None, :]).astype(jnp.int32), axis=0)
    return (chosen, blocks)


def draw_adapter_of_block(key, part):
    chosen, blocks = adapter_plan(key)
    return chosen


def draw_counts(key, part):
    chosen, blocks = adapter_plan(key)
    key = jax.random.fold_in(key, 5)
    padding = jax.random.randint(key, (ADAPTER_TOTAL,), 0, BLK)
    labels = jnp.arange(ADAPTER_TOTAL, dtype=jnp.int32)
    padding = jnp.where(labels == ADAPTER_TOTAL - 1, 0, padding)
    return jnp.where(blocks > 0, blocks * BLK - padding, 0).astype(jnp.int32)


def shard_levels(stream_key, extent, cuts, smallest, top_value):
    gain = 1.0
    for axis_at, shards_of in cuts:
        draws = jax.random.uniform(jax.random.fold_in(jax.random.fold_in(stream_key, 6), axis_at), (shards_of,), jnp.float32, smallest / len(cuts), top_value / len(cuts))
        gain = gain * jnp.repeat(jnp.exp(draws), extent[axis_at] // shards_of).reshape((-1,) + (1,) * (len(extent) - 1 - axis_at))
    return gain


def noise(stream_key, extent, width, reach, pieces=(), kind=jnp.bfloat16):
    values = width * jax.random.normal(stream_key, extent, jnp.float32)
    if pieces:
        values = values * shard_levels(stream_key, extent, pieces, -0.22, 0.18)
    return jnp.clip(values, -reach, reach).astype(kind)


def setup_inputs(seed: int = 0, part: int = 0) -> dict:
    key_list = jax.random.split(jax.random.key(seed), 8)
    part_splits = jax.random.split(jax.random.fold_in(key_list[7], part), 8)
    return {
        "activations": noise(part_splits[0], (TOKENS, INPUT_FEATURES), 1.0, 6.0, ((0, 8), (1, 2))),
        "cotangent": noise(part_splits[1], (TOKENS, HIDDEN_WIDTH), 0.0065, 0.039794922, ((0, 8), (1, 2))),
        "adapter_down_factors": noise(key_list[2], (ADAPTER_TOTAL, INPUT_FEATURES, ADAPTER_RANK), 0.3, 1.796875, ((0, 8), (1, 2))),
        "adapter_up_factors": noise(key_list[3], (ADAPTER_TOTAL, HIDDEN_WIDTH, ADAPTER_RANK), 0.15, 0.8984375, ((0, 8), (1, 2))),
        "adapter_slot": jax.random.permutation(key_list[4], ADAPTER_TOTAL).astype(jnp.int32),
        "adapter_of_block": draw_adapter_of_block(jax.random.fold_in(jax.random.fold_in(key_list[7], part), 71), part),
        "counts": draw_counts(jax.random.fold_in(jax.random.fold_in(key_list[7], part), 71), part),
    }


adapter_scale = 2.0


def row_plan(adapter_of_block, counts, adapter_slot):
    labels = jnp.arange(counts.shape[0], dtype=jnp.int32)
    matches = adapter_of_block[:, None] == labels[None, :]
    slot_of_block = jnp.sum(jnp.where(matches, adapter_slot[None, :], 0), axis=1).astype(jnp.int32)
    block_count = jnp.sum(jnp.where(matches, counts[None, :], 0), axis=1)
    order = jnp.arange(adapter_of_block.shape[0], dtype=jnp.int32)
    same_adapter = adapter_of_block[:, None] == adapter_of_block[None, :]
    earlier = jnp.sum(jnp.where(same_adapter & (order[None, :] < order[:, None]), 1, 0), axis=1)
    places = jnp.arange(BLK, dtype=jnp.int32)
    active_rows = jnp.where(earlier[:, None] * BLK + places[None, :] < block_count[:, None], 1.0, 0.0).astype(jnp.float32)
    return active_rows, slot_of_block


def reference(activations, cotangent, adapter_down_factors, adapter_up_factors, adapter_slot, adapter_of_block, counts):
    active_rows, slot_of_block = row_plan(adapter_of_block, counts, adapter_slot)
    inputs = activations.reshape(NBLOCKS, BLK, INPUT_FEATURES).astype(jnp.float32)
    factor_gradients = cotangent.reshape(NBLOCKS, BLK, HIDDEN_WIDTH).astype(jnp.float32)
    down_factor_blocks = adapter_down_factors[slot_of_block].astype(jnp.float32)
    up_factor_blocks = adapter_up_factors[slot_of_block].astype(jnp.float32)
    down_sum = jnp.einsum("btc,bcr->btr", inputs, down_factor_blocks)
    up_partial_sum = jnp.einsum("btc,bcr->btr", factor_gradients, up_factor_blocks)
    reduced_down = (active_rows[:, :, None] * down_sum).astype(jnp.bfloat16).astype(jnp.float32)
    reduced_up = (adapter_scale * active_rows[:, :, None] * up_partial_sum).astype(jnp.bfloat16).astype(jnp.float32)
    up_contributions = adapter_scale * jnp.einsum("eqi,eqf->eif", factor_gradients, reduced_down)
    grad_up = jax.ops.segment_sum(up_contributions, slot_of_block, num_segments=ADAPTER_TOTAL).astype(jnp.bfloat16)
    down_terms = jnp.einsum("eqi,eqf->eif", inputs, reduced_up)
    grad_down = jax.ops.segment_sum(down_terms, slot_of_block, num_segments=ADAPTER_TOTAL).astype(jnp.bfloat16)
    input_grad = jnp.einsum("btr,bcr->btc", reduced_up, down_factor_blocks).reshape(TOKENS, INPUT_FEATURES).astype(jnp.bfloat16)
    return input_grad, grad_down, grad_up
```

```python
import jax
import jax.numpy as jnp
from jax import lax
from jax.sharding import PartitionSpec as P

BLK = 128


adapter_scale = 2.0


def row_plan(adapter_of_block, counts, adapter_slot):
    labels = jnp.arange(counts.shape[0], dtype=jnp.int32)
    matches = adapter_of_block[:, None] == labels[None, :]
    slot_of_block = jnp.sum(jnp.where(matches, adapter_slot[None, :], 0), axis=1)
    block_count = jnp.sum(jnp.where(matches, counts[None, :], 0), axis=1)
    order = jnp.arange(adapter_of_block.shape[0], dtype=jnp.int32)
    same_adapter = adapter_of_block[:, None] == adapter_of_block[None, :]
    earlier = jnp.sum(jnp.where(same_adapter & (order[None, :] < order[:, None]), 1, 0), axis=1)
    places = jnp.arange(BLK, dtype=jnp.int32)
    active_rows = jnp.where(
        earlier[:, None] * BLK + places[None, :] < block_count[:, None], 1.0, 0.0
    ).astype(jnp.float32)
    return (active_rows, slot_of_block)


def rank_terms(columns, factor_blocks, nblocks):
    pieces = columns.reshape(nblocks, BLK, columns.shape[1])
    return jnp.einsum("btc,bcr->btr", pieces, factor_blocks, preferred_element_type=jnp.float32)


def slot_total(selector, terms, slots):
    flat = terms.reshape(terms.shape[0], -1)
    summed = jnp.dot(
        selector, flat, precision=lax.Precision.HIGHEST, preferred_element_type=jnp.float32
    )
    return summed.reshape(slots, terms.shape[1], terms.shape[2]).astype(jnp.bfloat16)


def on_device(
    activations,
    cotangent,
    adapter_down_factors,
    adapter_up_factors,
    adapter_slot,
    adapter_of_block,
    counts,
):
    nblocks = adapter_of_block.shape[0]
    slots = adapter_slot.shape[0]
    active_rows, slot_of_block = row_plan(adapter_of_block, counts, adapter_slot)
    selector = (slot_of_block[None, :] == jnp.arange(slots, dtype=jnp.int32)[:, None]).astype(
        jnp.float32
    )
    down_cols, up_cols = (
        lax.all_to_all(adapter_down_factors, "rows", split_axis=1, concat_axis=0, tiled=True),
        lax.all_to_all(adapter_up_factors, "rows", split_axis=1, concat_axis=0, tiled=True),
    )
    down_factor_blocks = down_cols[slot_of_block]
    up_factor_blocks = up_cols[slot_of_block]
    input_cols, grad_cols = (
        lax.all_to_all(activations, "rows", split_axis=1, concat_axis=0, tiled=True),
        lax.all_to_all(cotangent, "rows", split_axis=1, concat_axis=0, tiled=True),
    )
    down_sum, up_partial_sum = lax.psum(
        (
            rank_terms(input_cols, down_factor_blocks, nblocks),
            rank_terms(grad_cols, up_factor_blocks, nblocks),
        ),
        ("rows", "tp"),
    )
    reduced_down = (active_rows[:, :, None] * down_sum).astype(jnp.bfloat16)
    reduced_up = (adapter_scale * active_rows[:, :, None] * up_partial_sum).astype(jnp.bfloat16)
    grad_pieces = grad_cols.reshape(nblocks, BLK, grad_cols.shape[1])
    input_pieces = input_cols.reshape(nblocks, BLK, input_cols.shape[1])
    up_contributions = adapter_scale * jnp.einsum(
        "eqi,eqf->eif", grad_pieces, reduced_down, preferred_element_type=jnp.float32
    )
    down_terms = jnp.einsum(
        "eqi,eqf->eif", input_pieces, reduced_up, preferred_element_type=jnp.float32
    )
    grad_up_cols = slot_total(selector, up_contributions, slots)
    grad_down_cols = slot_total(selector, down_terms, slots)
    input_grad_cols = jnp.einsum(
        "btr,bcr->btc", reduced_up, down_factor_blocks, preferred_element_type=jnp.float32
    )
    input_grad_cols = input_grad_cols.reshape(nblocks * BLK, input_cols.shape[1]).astype(
        jnp.bfloat16
    )
    input_grad, grad_down, grad_up = (
        lax.all_to_all(input_grad_cols, "rows", split_axis=0, concat_axis=1, tiled=True),
        lax.all_to_all(grad_down_cols, "rows", split_axis=0, concat_axis=1, tiled=True),
        lax.all_to_all(grad_up_cols, "rows", split_axis=0, concat_axis=1, tiled=True),
    )
    return (input_grad, grad_down, grad_up)


GATHER_LIMIT = 24 << 20


def tenant_plan(
    activations,
    cotangent,
    adapter_down_factors,
    adapter_up_factors,
    adapter_slot,
    adapter_of_block,
    counts,
):
    active_rows, slot_of_block = row_plan(adapter_of_block, counts, adapter_slot)
    me = lax.axis_index("rows")
    inputs = activations.shape[1]
    mine = jnp.concatenate(
        [jnp.swapaxes(adapter_down_factors, 1, 2), jnp.swapaxes(adapter_up_factors, 1, 2)], axis=2
    )
    factors = lax.all_gather(mine, "rows", axis=0, tiled=True)
    factor = lax.dynamic_index_in_dim(factors, slot_of_block[me], 0, keepdims=False)
    live = lax.dynamic_index_in_dim(active_rows, me, 0, keepdims=False)[:, None]
    sums = jnp.concatenate(
        [
            lax.dot_general(activations, factor[:, :inputs], (((1,), (1,)), ((), ())),
                            preferred_element_type=jnp.float32),
            lax.dot_general(cotangent, factor[:, inputs:], (((1,), (1,)), ((), ())),
                            preferred_element_type=jnp.float32),
        ],
        axis=1,
    )
    sums = lax.psum(sums, "tp")
    rank = factor.shape[0]
    low_down = (live * sums[:, :rank]).astype(jnp.bfloat16)
    low_up = (adapter_scale * live * sums[:, rank:]).astype(jnp.bfloat16)
    input_grad = jnp.dot(low_up, factor[:, :inputs], preferred_element_type=jnp.float32)
    over_rows = (((0,), (0,)), ((), ()))
    terms = jnp.concatenate(
        [
            lax.dot_general(low_up, activations, over_rows, preferred_element_type=jnp.float32),
            adapter_scale
            * lax.dot_general(low_down, cotangent, over_rows, preferred_element_type=jnp.float32),
        ],
        axis=1,
    ).astype(jnp.bfloat16)
    every = lax.all_gather(terms, "rows", axis=0, tiled=False).astype(jnp.float32)
    here = adapter_down_factors.shape[0]
    grads = jnp.stack(
        [
            jnp.sum(
                jnp.where((slot_of_block == me * here + at)[:, None, None], every, 0.0), axis=0
            )
            for at in range(here)
        ]
    ).astype(jnp.bfloat16)
    return (
        input_grad.astype(jnp.bfloat16),
        jnp.swapaxes(grads[:, :, :inputs], 1, 2),
        jnp.swapaxes(grads[:, :, inputs:], 1, 2),
    )


def choose(*args):
    factors = (args[2].size + args[3].size) * 2 * jax.lax.axis_size("rows")
    one_block = args[0].shape[0] == BLK
    plan = tenant_plan if one_block and factors <= GATHER_LIMIT else on_device
    return plan(*args)


def solution(mesh):
    in_specs = (
        P(("groups", "rows"), "tp"),
        P(("groups", "rows"), "tp"),
        P("rows", "tp", None),
        P("rows", "tp", None),
        P(),
        P("groups"),
        P("groups"),
    )
    out_specs = (
        P(("groups", "rows"), "tp"),
        P(("groups", "rows"), "tp", None),
        P(("groups", "rows"), "tp", None),
    )
    return jax.shard_map(
        choose, mesh=mesh, in_specs=in_specs, out_specs=out_specs, check_vma=False
    )
```

```python
import functools

import jax
import jax.numpy as jnp
from jax import lax
from jax.experimental import pallas as pl
from jax.experimental.pallas import tpu as pltpu
from jax.sharding import PartitionSpec as P

BLK = 128


adapter_scale = 2.0


def row_plan(adapter_of_block, counts, adapter_slot):
    labels = jnp.arange(counts.shape[0], dtype=jnp.int32)
    matches = adapter_of_block[:, None] == labels[None, :]
    slot_of_block = jnp.sum(jnp.where(matches, adapter_slot[None, :], 0), axis=1)
    block_count = jnp.sum(jnp.where(matches, counts[None, :], 0), axis=1)
    order = jnp.arange(adapter_of_block.shape[0], dtype=jnp.int32)
    same_adapter = adapter_of_block[:, None] == adapter_of_block[None, :]
    earlier = jnp.sum(jnp.where(same_adapter & (order[None, :] < order[:, None]), 1, 0), axis=1)
    places = jnp.arange(BLK, dtype=jnp.int32)
    active_rows = jnp.where(
        earlier[:, None] * BLK + places[None, :] < block_count[:, None], 1.0, 0.0
    ).astype(jnp.float32)
    return (active_rows, slot_of_block)


def rank_terms(columns, factor_blocks, nblocks):
    pieces = columns.reshape(nblocks, BLK, columns.shape[1])
    return jnp.einsum("btc,bcr->btr", pieces, factor_blocks, preferred_element_type=jnp.float32)


def slot_total(selector, terms, slots):
    flat = terms.reshape(terms.shape[0], -1)
    summed = jnp.dot(
        selector, flat, precision=lax.Precision.HIGHEST, preferred_element_type=jnp.float32
    )
    return summed.reshape(slots, terms.shape[1], terms.shape[2]).astype(jnp.bfloat16)


def on_device(
    activations,
    cotangent,
    adapter_down_factors,
    adapter_up_factors,
    adapter_slot,
    adapter_of_block,
    counts,
):
    nblocks = adapter_of_block.shape[0]
    slots = adapter_slot.shape[0]
    active_rows, slot_of_block = row_plan(adapter_of_block, counts, adapter_slot)
    selector = (slot_of_block[None, :] == jnp.arange(slots, dtype=jnp.int32)[:, None]).astype(
        jnp.float32
    )
    down_cols, up_cols = (
        lax.all_to_all(adapter_down_factors, "rows", split_axis=1, concat_axis=0, tiled=True),
        lax.all_to_all(adapter_up_factors, "rows", split_axis=1, concat_axis=0, tiled=True),
    )
    down_factor_blocks = down_cols[slot_of_block]
    up_factor_blocks = up_cols[slot_of_block]
    input_cols, grad_cols = (
        lax.all_to_all(activations, "rows", split_axis=1, concat_axis=0, tiled=True),
        lax.all_to_all(cotangent, "rows", split_axis=1, concat_axis=0, tiled=True),
    )
    down_sum, up_partial_sum = lax.psum(
        (
            rank_terms(input_cols, down_factor_blocks, nblocks),
            rank_terms(grad_cols, up_factor_blocks, nblocks),
        ),
        ("rows", "tp"),
    )
    reduced_down = (active_rows[:, :, None] * down_sum).astype(jnp.bfloat16)
    reduced_up = (adapter_scale * active_rows[:, :, None] * up_partial_sum).astype(jnp.bfloat16)
    grad_pieces = grad_cols.reshape(nblocks, BLK, grad_cols.shape[1])
    input_pieces = input_cols.reshape(nblocks, BLK, input_cols.shape[1])
    up_contributions = adapter_scale * jnp.einsum(
        "eqi,eqf->eif", grad_pieces, reduced_down, preferred_element_type=jnp.float32
    )
    down_terms = jnp.einsum(
        "eqi,eqf->eif", input_pieces, reduced_up, preferred_element_type=jnp.float32
    )
    grad_up_cols = slot_total(selector, up_contributions, slots)
    grad_down_cols = slot_total(selector, down_terms, slots)
    input_grad_cols = jnp.einsum(
        "btr,bcr->btc", reduced_up, down_factor_blocks, preferred_element_type=jnp.float32
    )
    input_grad_cols = input_grad_cols.reshape(nblocks * BLK, input_cols.shape[1]).astype(
        jnp.bfloat16
    )
    input_grad, grad_down, grad_up = (
        lax.all_to_all(input_grad_cols, "rows", split_axis=0, concat_axis=1, tiled=True),
        lax.all_to_all(grad_down_cols, "rows", split_axis=0, concat_axis=1, tiled=True),
        lax.all_to_all(grad_up_cols, "rows", split_axis=0, concat_axis=1, tiled=True),
    )
    return (input_grad, grad_down, grad_up)


GATHER_LIMIT = 24 << 20


LANES = 2
MESH = pl.DeviceIdType.MESH
NT = (((1,), (1,)), ((), ()))
TN = (((0,), (0,)), ((), ()))


def line_gather(buf, piece, send, recv, rows):
    line = rows // LANES
    me = lax.axis_index("rows")
    at, lane = me // LANES, me % LANES

    def copy(where, p, to):
        return pltpu.make_async_remote_copy(
            src_ref=piece(buf, p),
            dst_ref=piece(buf, p),
            send_sem=send.at[where, p // LANES],
            recv_sem=recv.at[p],
            device_id={"rows": to},
            device_id_type=MESH,
        )

    def arrived(p):
        copy(0, p, me ^ 1).wait_recv()

    def start():
        @pl.when(at < line - 1)
        def _():
            copy(0, me, me + LANES).start()

        @pl.when(at > 0)
        def _():
            copy(1, me, me - LANES).start()

        copy(2, me, me ^ 1).start()

    def forward():
        for k in range(1, line):
            low, high = me - k * LANES, me + k * LANES

            @pl.when(at - k >= 0)
            def _():
                arrived(low)

                @pl.when(at < line - 1)
                def _():
                    copy(0, low, me + LANES).start()

                copy(2, low, me ^ 1).start()

            @pl.when(at + k < line)
            def _():
                arrived(high)

                @pl.when(at > 0)
                def _():
                    copy(1, high, me - LANES).start()

                copy(2, high, me ^ 1).start()

        for z in range(line):
            arrived(z * LANES + 1 - lane)

    def drain():
        for z in range(line):
            p = z * LANES + lane
            copy(2, p, me ^ 1).wait_send()

            @pl.when(jnp.logical_and(z <= at, at < line - 1))
            def _():
                copy(0, p, me + LANES).wait_send()

            @pl.when(jnp.logical_and(z >= at, at > 0))
            def _():
                copy(1, p, me - LANES).wait_send()

    return start, forward, drain


def tenant_kernel(
    rows,
    wanted,
    block_slots,
    live,
    mine,
    act_hbm,
    cot_hbm,
    input_grad,
    grad_down,
    grad_up,
    fac,
    terms,
    act,
    cot,
    half_out,
    half_in,
    sum_out,
    sum_in,
    fac_send,
    fac_recv,
    term_send,
    term_recv,
    pair_send,
    pair_recv,
    local,
):
    me = lax.axis_index("rows")
    group = lax.axis_index("groups")
    core = lax.axis_index("tp")
    line = rows // LANES
    at = me // LANES
    here = mine.shape[0]
    inputs = act.shape[1]
    hidden = cot.shape[1]
    ih, hh = inputs // 2, hidden // 2

    loads = [
        pltpu.make_async_copy(act_hbm, act, local.at[0]),
        pltpu.make_async_copy(cot_hbm, cot, local.at[1]),
    ]
    for load in loads:
        load.start()
    fac[pl.ds(me * here, here)] = mine[...]

    barrier = pltpu.get_barrier_semaphore()

    def greet(target):
        pl.semaphore_signal(barrier, inc=1, device_id=target, device_id_type=MESH)

    greet({"rows": me ^ 1})
    greet({"groups": 1 - group})
    greet({"tp": 1 - core})

    @pl.when(at > 0)
    def _():
        greet({"rows": me - LANES})

    @pl.when(at < line - 1)
    def _():
        greet({"rows": me + LANES})

    pl.semaphore_wait(
        barrier, 3 + jnp.where(at > 0, 1, 0) + jnp.where(at < line - 1, 1, 0)
    )

    start, forward, drain = line_gather(
        fac, lambda r, p: r.at[pl.ds(p * here, here)], fac_send, fac_recv, rows
    )
    start()
    forward()

    half_out[...] = fac[wanted[1]]
    swap = pltpu.make_async_remote_copy(
        src_ref=half_out,
        dst_ref=half_in,
        send_sem=pair_send.at[0],
        recv_sem=pair_recv.at[0],
        device_id={"groups": 1 - group},
        device_id_type=MESH,
    )
    swap.start()
    own = fac[wanted[0]]
    for load in loads:
        load.wait()
    swap.wait_recv()
    other = half_in[...]
    first = group == 0
    left = jnp.where(first, own, other)
    right = jnp.where(first, other, own)

    def dot(a, b, dims=(((1,), (0,)), ((), ()))):
        return lax.dot_general(a, b, dims, preferred_element_type=jnp.float32)

    rank = left.shape[0]
    sum_out[0:rank] = dot(left[:, :ih], act[:, :ih], NT) + dot(right[:, :ih], act[:, ih:], NT)
    sum_out[rank:] = dot(left[:, ih:], cot[:, :hh], NT) + dot(right[:, ih:], cot[:, hh:], NT)
    pair = pltpu.make_async_remote_copy(
        src_ref=sum_out,
        dst_ref=sum_in,
        send_sem=pair_send.at[1],
        recv_sem=pair_recv.at[1],
        device_id={"tp": 1 - core},
        device_id_type=MESH,
    )
    pair.start()
    pair.wait_recv()
    sums = sum_out[...] + sum_in[...]
    low_down = (live[...] * sums[:rank]).astype(jnp.bfloat16)
    low_up = (adapter_scale * live[...] * sums[rank:]).astype(jnp.bfloat16)

    terms[me, :, 0:inputs] = dot(low_up, act[...]).astype(jnp.bfloat16)
    terms[me, :, inputs:] = (adapter_scale * dot(low_down, cot[...])).astype(jnp.bfloat16)
    start2, forward2, drain2 = line_gather(
        terms, lambda r, p: r.at[p], term_send, term_recv, rows
    )
    start2()
    input_grad[:, 0:ih] = dot(low_up, left[:, :ih], TN).astype(jnp.bfloat16)
    input_grad[:, ih:] = dot(low_up, right[:, :ih], TN).astype(jnp.bfloat16)
    forward2()

    tile = 512
    for out, base, width in ((grad_down, 0, inputs), (grad_up, inputs, hidden)):

        def add(i, carry, out=out, base=base):
            to = pl.ds(pl.multiple_of(i * tile, tile), tile)
            source = pl.ds(pl.multiple_of(base + i * tile, tile), tile)
            totals = [jnp.zeros((rank, tile), jnp.float32) for _ in range(here)]
            for b in range(rows):
                term = terms[b, :, source].astype(jnp.float32)
                for j in range(here):
                    mask = jnp.where(block_slots[b] == me * here + j, 1.0, 0.0)
                    totals[j] += mask * term
            for j in range(here):
                out[j, :, to] = totals[j].astype(jnp.bfloat16)
            return carry

        lax.fori_loop(0, width // tile, add, 0)

    drain()
    drain2()
    swap.wait_send()
    pair.wait_send()


def tenant_plan(
    activations,
    cotangent,
    adapter_down_factors,
    adapter_up_factors,
    adapter_slot,
    adapter_of_block,
    counts,
):
    active_rows, slot_of_block = row_plan(adapter_of_block, counts, adapter_slot)
    rows = jax.lax.axis_size("rows")
    me = lax.axis_index("rows")
    group = lax.axis_index("groups")
    here, inputs, rank = adapter_down_factors.shape
    hidden = adapter_up_factors.shape[1]
    half = (inputs + hidden) // 2
    down = jnp.swapaxes(adapter_down_factors, 1, 2)
    up = jnp.swapaxes(adapter_up_factors, 1, 2)
    mine = jnp.concatenate(
        [
            lax.dynamic_slice_in_dim(down, group * (inputs // 2), inputs // 2, 2),
            lax.dynamic_slice_in_dim(up, group * (hidden // 2), hidden // 2, 2),
        ],
        axis=2,
    )
    slot = slot_of_block[me]
    both = lax.all_gather(slot_of_block, "groups")
    wanted = jnp.stack([slot, both[1 - group, me]])
    live = lax.dynamic_slice_in_dim(active_rows, me, 1, 0)
    bf16, f32 = jnp.bfloat16, jnp.float32
    line = rows // LANES
    vmem = pl.BlockSpec(memory_space=pltpu.VMEM)
    smem = pl.BlockSpec(memory_space=pltpu.SMEM)
    hbm = pl.BlockSpec(memory_space=pl.ANY)
    dma = pltpu.SemaphoreType.DMA
    input_grad, grad_down, grad_up = pl.pallas_call(
        functools.partial(tenant_kernel, rows),
        out_shape=(
            jax.ShapeDtypeStruct((BLK, inputs), bf16),
            jax.ShapeDtypeStruct((here, rank, inputs), bf16),
            jax.ShapeDtypeStruct((here, rank, hidden), bf16),
        ),
        in_specs=[smem, smem, vmem, vmem, hbm, hbm],
        out_specs=(vmem, vmem, vmem),
        scratch_shapes=[
            pltpu.VMEM((rows * here, rank, half), bf16),
            pltpu.VMEM((rows, rank, inputs + hidden), bf16),
            pltpu.VMEM((BLK, inputs), bf16),
            pltpu.VMEM((BLK, hidden), bf16),
            pltpu.VMEM((rank, half), bf16),
            pltpu.VMEM((rank, half), bf16),
            pltpu.VMEM((2 * rank, BLK), f32),
            pltpu.VMEM((2 * rank, BLK), f32),
            dma((3, line)),
            dma((rows,)),
            dma((3, line)),
            dma((rows,)),
            dma((2,)),
            dma((2,)),
            dma((2,)),
        ],
        compiler_params=pltpu.CompilerParams(
            collective_id=0, has_side_effects=True, vmem_limit_bytes=40 << 20
        ),
    )(wanted, slot_of_block, live, mine, activations, cotangent)
    return input_grad, jnp.swapaxes(grad_down, 1, 2), jnp.swapaxes(grad_up, 1, 2)


def choose(*args):
    factors = (args[2].size + args[3].size) * 2 * jax.lax.axis_size("rows")
    one_block = args[0].shape[0] == BLK
    plan = tenant_plan if one_block and jax.lax.axis_size("groups") == 2 and factors <= GATHER_LIMIT else on_device
    return plan(*args)


def solution(mesh):
    in_specs = (
        P(("groups", "rows"), "tp"),
        P(("groups", "rows"), "tp"),
        P("rows", "tp", None),
        P("rows", "tp", None),
        P(),
        P("groups"),
        P("groups"),
    )
    out_specs = (
        P(("groups", "rows"), "tp"),
        P(("groups", "rows"), "tp", None),
        P(("groups", "rows"), "tp", None),
    )
    return jax.shard_map(
        choose, mesh=mesh, in_specs=in_specs, out_specs=out_specs, check_vma=False
    )
```

```python
import functools

import jax
import jax.numpy as jnp
from jax import lax
from jax.experimental import pallas as pl
from jax.experimental.pallas import tpu as pltpu
from jax.sharding import PartitionSpec as P

BLK = 128


adapter_scale = 2.0


def row_plan(adapter_of_block, counts, adapter_slot):
    labels = jnp.arange(counts.shape[0], dtype=jnp.int32)
    matches = adapter_of_block[:, None] == labels[None, :]
    slot_of_block = jnp.sum(jnp.where(matches, adapter_slot[None, :], 0), axis=1)
    block_count = jnp.sum(jnp.where(matches, counts[None, :], 0), axis=1)
    order = jnp.arange(adapter_of_block.shape[0], dtype=jnp.int32)
    same_adapter = adapter_of_block[:, None] == adapter_of_block[None, :]
    earlier = jnp.sum(jnp.where(same_adapter & (order[None, :] < order[:, None]), 1, 0), axis=1)
    places = jnp.arange(BLK, dtype=jnp.int32)
    active_rows = jnp.where(
        earlier[:, None] * BLK + places[None, :] < block_count[:, None], 1.0, 0.0
    ).astype(jnp.float32)
    return (active_rows, slot_of_block)


def rank_terms(columns, factor_blocks, nblocks):
    pieces = columns.reshape(nblocks, BLK, columns.shape[1])
    return jnp.einsum("btc,bcr->btr", pieces, factor_blocks, preferred_element_type=jnp.float32)


def slot_total(selector, terms, slots):
    flat = terms.reshape(terms.shape[0], -1)
    summed = jnp.dot(
        selector, flat, precision=lax.Precision.HIGHEST, preferred_element_type=jnp.float32
    )
    return summed.reshape(slots, terms.shape[1], terms.shape[2]).astype(jnp.bfloat16)


def on_device(
    activations,
    cotangent,
    adapter_down_factors,
    adapter_up_factors,
    adapter_slot,
    adapter_of_block,
    counts,
):
    nblocks = adapter_of_block.shape[0]
    slots = adapter_slot.shape[0]
    active_rows, slot_of_block = row_plan(adapter_of_block, counts, adapter_slot)
    selector = (slot_of_block[None, :] == jnp.arange(slots, dtype=jnp.int32)[:, None]).astype(
        jnp.float32
    )
    down_cols, up_cols = (
        lax.all_to_all(adapter_down_factors, "rows", split_axis=1, concat_axis=0, tiled=True),
        lax.all_to_all(adapter_up_factors, "rows", split_axis=1, concat_axis=0, tiled=True),
    )
    down_factor_blocks = down_cols[slot_of_block]
    up_factor_blocks = up_cols[slot_of_block]
    input_cols, grad_cols = (
        lax.all_to_all(activations, "rows", split_axis=1, concat_axis=0, tiled=True),
        lax.all_to_all(cotangent, "rows", split_axis=1, concat_axis=0, tiled=True),
    )
    down_sum, up_partial_sum = lax.psum(
        (
            rank_terms(input_cols, down_factor_blocks, nblocks),
            rank_terms(grad_cols, up_factor_blocks, nblocks),
        ),
        ("rows", "tp"),
    )
    reduced_down = (active_rows[:, :, None] * down_sum).astype(jnp.bfloat16)
    reduced_up = (adapter_scale * active_rows[:, :, None] * up_partial_sum).astype(jnp.bfloat16)
    grad_pieces = grad_cols.reshape(nblocks, BLK, grad_cols.shape[1])
    input_pieces = input_cols.reshape(nblocks, BLK, input_cols.shape[1])
    up_contributions = adapter_scale * jnp.einsum(
        "eqi,eqf->eif", grad_pieces, reduced_down, preferred_element_type=jnp.float32
    )
    down_terms = jnp.einsum(
        "eqi,eqf->eif", input_pieces, reduced_up, preferred_element_type=jnp.float32
    )
    grad_up_cols = slot_total(selector, up_contributions, slots)
    grad_down_cols = slot_total(selector, down_terms, slots)
    input_grad_cols = jnp.einsum(
        "btr,bcr->btc", reduced_up, down_factor_blocks, preferred_element_type=jnp.float32
    )
    input_grad_cols = input_grad_cols.reshape(nblocks * BLK, input_cols.shape[1]).astype(
        jnp.bfloat16
    )
    input_grad, grad_down, grad_up = (
        lax.all_to_all(input_grad_cols, "rows", split_axis=0, concat_axis=1, tiled=True),
        lax.all_to_all(grad_down_cols, "rows", split_axis=0, concat_axis=1, tiled=True),
        lax.all_to_all(grad_up_cols, "rows", split_axis=0, concat_axis=1, tiled=True),
    )
    return (input_grad, grad_down, grad_up)


GATHER_LIMIT = 24 << 20


LANES = 2
MESH = pl.DeviceIdType.MESH
NT = (((1,), (1,)), ((), ()))
TN = (((0,), (0,)), ((), ()))


def line_gather(buf, piece, send, recv, rows):
    line = rows // LANES
    me = lax.axis_index("rows")
    at, lane = me // LANES, me % LANES

    def copy(where, p, to):
        return pltpu.make_async_remote_copy(
            src_ref=piece(buf, p),
            dst_ref=piece(buf, p),
            send_sem=send.at[where, p // LANES],
            recv_sem=recv.at[p],
            device_id={"rows": to},
            device_id_type=MESH,
        )

    def arrived(p):
        copy(0, p, me ^ 1).wait_recv()

    def start():
        @pl.when(at < line - 1)
        def _():
            copy(0, me, me + LANES).start()

        @pl.when(at > 0)
        def _():
            copy(1, me, me - LANES).start()

        copy(2, me, me ^ 1).start()

    def forward():
        for k in range(1, line):
            low, high = me - k * LANES, me + k * LANES

            @pl.when(at - k >= 0)
            def _():
                arrived(low)

                @pl.when(at < line - 1)
                def _():
                    copy(0, low, me + LANES).start()

                copy(2, low, me ^ 1).start()

            @pl.when(at + k < line)
            def _():
                arrived(high)

                @pl.when(at > 0)
                def _():
                    copy(1, high, me - LANES).start()

                copy(2, high, me ^ 1).start()

    def beside():
        for z in range(line):
            arrived(z * LANES + 1 - lane)

    def drain():
        for z in range(line):
            p = z * LANES + lane
            copy(2, p, me ^ 1).wait_send()

            @pl.when(jnp.logical_and(z <= at, at < line - 1))
            def _():
                copy(0, p, me + LANES).wait_send()

            @pl.when(jnp.logical_and(z >= at, at > 0))
            def _():
                copy(1, p, me - LANES).wait_send()

    return start, forward, beside, drain


def tenant_kernel(
    rows,
    slot_of,
    block_adapter,
    counts,
    down_hbm,
    up_hbm,
    act_hbm,
    cot_hbm,
    input_grad,
    grad_down,
    grad_up,
    fac,
    terms,
    totals,
    act,
    cot,
    half_out,
    half_in,
    sum_out,
    sum_in,
    wish_out,
    wish_in,
    wish,
    fac_send,
    fac_recv,
    term_send,
    term_recv,
    pair_send,
    pair_recv,
    local,
):
    me = lax.axis_index("rows")
    group = lax.axis_index("groups")
    core = lax.axis_index("tp")
    line = rows // LANES
    at, lane = me // LANES, me % LANES
    here, rank, inputs = grad_down.shape
    hidden = cot.shape[1]
    ih, hh = inputs // 2, hidden // 2
    spot = pl.ds(me * here, here)

    own_factors = [
        pltpu.make_async_copy(
            down_hbm.at[:, :, pl.ds(pl.multiple_of(group * ih, 128), ih)],
            fac.at[spot, :, pl.ds(0, ih)],
            local.at[2],
        ),
        pltpu.make_async_copy(
            up_hbm.at[:, :, pl.ds(pl.multiple_of(group * hh, 128), hh)],
            fac.at[spot, :, pl.ds(ih, hh)],
            local.at[3],
        ),
    ]
    for load in own_factors:
        load.start()
    loads = [
        pltpu.make_async_copy(act_hbm, act, local.at[0]),
        pltpu.make_async_copy(cot_hbm, cot, local.at[1]),
    ]
    for load in loads:
        load.start()

    barrier = pltpu.get_barrier_semaphore()

    def greet(target):
        pl.semaphore_signal(barrier, inc=1, device_id=target, device_id_type=MESH)

    greet({"rows": me ^ 1})
    greet({"groups": 1 - group})
    greet({"tp": 1 - core})

    @pl.when(at > 0)
    def _():
        greet({"rows": me - LANES})

    @pl.when(at < line - 1)
    def _():
        greet({"rows": me + LANES})

    adapter = block_adapter[me]
    slot = slot_of[adapter]
    earlier = jnp.int32(0)
    for b in range(rows):
        same = jnp.logical_and(block_adapter[b] == adapter, b < me)
        earlier += jnp.where(same, 1, 0)
    place = lax.broadcasted_iota(jnp.int32, (1, BLK), 1)
    live = jnp.where(earlier * BLK + place < counts[adapter], 1.0, 0.0)
    wish_out[...] = jnp.full(wish_out.shape, slot, jnp.int32)

    for load in own_factors:
        load.wait()
    pl.semaphore_wait(
        barrier, 3 + jnp.where(at > 0, 1, 0) + jnp.where(at < line - 1, 1, 0)
    )

    def pair(source, target, which, to):
        return pltpu.make_async_remote_copy(
            src_ref=source,
            dst_ref=target,
            send_sem=pair_send.at[which],
            recv_sem=pair_recv.at[which],
            device_id=to,
            device_id_type=MESH,
        )

    start, forward, beside, drain = line_gather(
        fac, lambda r, p: r.at[pl.ds(p * here, here)], fac_send, fac_recv, rows
    )
    start()
    ask = pair(wish_out, wish_in, 2, {"groups": 1 - group})
    ask.start()
    forward()
    ask.wait_recv()
    note = pltpu.make_async_copy(wish_in, wish, local.at[4])
    note.start()
    note.wait()
    for load in loads:
        load.wait()
    beside()

    half_out[...] = fac[wish[0, 0]]
    swap = pair(half_out, half_in, 0, {"groups": 1 - group})
    swap.start()

    def dot(a, b, dims=(((1,), (0,)), ((), ()))):
        return lax.dot_general(a, b, dims, preferred_element_type=jnp.float32)

    def part(index, width):
        return pl.ds(pl.multiple_of(index * width, 128), width)

    own = fac[slot]
    own_down = dot(own[:, :ih], act[:, part(group, ih)], NT)
    own_up = dot(own[:, ih:], cot[:, part(group, hh)], NT)
    swap.wait_recv()
    other = half_in[...]
    sum_out[0:rank] = own_down + dot(other[:, :ih], act[:, part(1 - group, ih)], NT)
    sum_out[rank:] = own_up + dot(other[:, ih:], cot[:, part(1 - group, hh)], NT)
    share = pair(sum_out, sum_in, 1, {"tp": 1 - core})
    share.start()
    share.wait_recv()
    sums = sum_out[...] + sum_in[...]
    low_down = (live * sums[:rank]).astype(jnp.bfloat16)
    low_up = (adapter_scale * live * sums[rank:]).astype(jnp.bfloat16)

    terms[me, :, 0:inputs] = dot(low_up, act[...]).astype(jnp.bfloat16)
    terms[me, :, inputs:] = (adapter_scale * dot(low_down, cot[...])).astype(jnp.bfloat16)
    start2, forward2, beside2, drain2 = line_gather(
        terms, lambda r, p: r.at[p], term_send, term_recv, rows
    )
    start2()
    input_grad[:, part(group, ih)] = dot(low_up, own[:, :ih], TN).astype(jnp.bfloat16)
    input_grad[:, part(1 - group, ih)] = dot(low_up, other[:, :ih], TN).astype(jnp.bfloat16)
    drain()
    forward2()

    tile = 512

    def weights(which):
        slots = [slot_of[block_adapter[z * LANES + which]] for z in range(line)]
        return [
            [jnp.where(s == me * here + j, 1.0, 0.0) for s in slots] for j in range(here)
        ]

    def add(which, mask, source, j):
        total = mask[j][0] * terms[which, :, source].astype(jnp.float32)
        for z in range(1, line):
            total += mask[j][z] * terms[z * LANES + which, :, source].astype(jnp.float32)
        return total

    same_lane = weights(lane)

    def first(i, carry):
        source = part(i, tile)
        for j in range(here):
            totals[j, :, source] = add(lane, same_lane, source, j)
        return carry

    lax.fori_loop(0, (inputs + hidden) // tile, first, 0)
    beside2()
    other_lane = weights(1 - lane)
    for out, base, width in ((grad_down, 0, inputs), (grad_up, inputs, hidden)):

        def second(i, carry, out=out, base=base):
            source = pl.ds(pl.multiple_of(base + i * tile, tile), tile)
            for j in range(here):
                total = totals[j, :, source] + add(1 - lane, other_lane, source, j)
                out[j, :, part(i, tile)] = total.astype(jnp.bfloat16)
            return carry

        lax.fori_loop(0, width // tile, second, 0)

    drain2()
    ask.wait_send()
    swap.wait_send()
    share.wait_send()


def tenant_plan(
    activations,
    cotangent,
    adapter_down_factors,
    adapter_up_factors,
    adapter_slot,
    adapter_of_block,
    counts,
):
    rows = jax.lax.axis_size("rows")
    here, inputs, rank = adapter_down_factors.shape
    hidden = adapter_up_factors.shape[1]
    half = (inputs + hidden) // 2
    bf16, f32, i32 = jnp.bfloat16, jnp.float32, jnp.int32
    line = rows // LANES
    vmem = pl.BlockSpec(memory_space=pltpu.VMEM)
    smem = pl.BlockSpec(memory_space=pltpu.SMEM)
    hbm = pl.BlockSpec(memory_space=pl.ANY)
    dma = pltpu.SemaphoreType.DMA
    input_grad, grad_down, grad_up = pl.pallas_call(
        functools.partial(tenant_kernel, rows),
        out_shape=(
            jax.ShapeDtypeStruct((BLK, inputs), bf16),
            jax.ShapeDtypeStruct((here, rank, inputs), bf16),
            jax.ShapeDtypeStruct((here, rank, hidden), bf16),
        ),
        in_specs=[smem, smem, smem, hbm, hbm, hbm, hbm],
        out_specs=(vmem, vmem, vmem),
        scratch_shapes=[
            pltpu.VMEM((rows * here, rank, half), bf16),
            pltpu.VMEM((rows, rank, inputs + hidden), bf16),
            pltpu.VMEM((here, rank, inputs + hidden), f32),
            pltpu.VMEM((BLK, inputs), bf16),
            pltpu.VMEM((BLK, hidden), bf16),
            pltpu.VMEM((rank, half), bf16),
            pltpu.VMEM((rank, half), bf16),
            pltpu.VMEM((2 * rank, BLK), f32),
            pltpu.VMEM((2 * rank, BLK), f32),
            pltpu.VMEM((8, 128), i32),
            pltpu.VMEM((8, 128), i32),
            pltpu.SMEM((8, 128), i32),
            dma((3, line)),
            dma((rows,)),
            dma((3, line)),
            dma((rows,)),
            dma((3,)),
            dma((3,)),
            dma((5,)),
        ],
        compiler_params=pltpu.CompilerParams(
            collective_id=0, has_side_effects=True, vmem_limit_bytes=40 << 20
        ),
    )(
        adapter_slot,
        adapter_of_block,
        counts,
        jnp.swapaxes(adapter_down_factors, 1, 2),
        jnp.swapaxes(adapter_up_factors, 1, 2),
        activations,
        cotangent,
    )
    return input_grad, jnp.swapaxes(grad_down, 1, 2), jnp.swapaxes(grad_up, 1, 2)


def choose(*args):
    factors = (args[2].size + args[3].size) * 2 * jax.lax.axis_size("rows")
    one_block = args[0].shape[0] == BLK
    plan = tenant_plan if one_block and jax.lax.axis_size("groups") == 2 and factors <= GATHER_LIMIT else on_device
    return plan(*args)


def solution(mesh):
    in_specs = (
        P(("groups", "rows"), "tp"),
        P(("groups", "rows"), "tp"),
        P("rows", "tp", None),
        P("rows", "tp", None),
        P(),
        P("groups"),
        P("groups"),
    )
    out_specs = (
        P(("groups", "rows"), "tp"),
        P(("groups", "rows"), "tp", None),
        P(("groups", "rows"), "tp", None),
    )
    return jax.shard_map(
        choose, mesh=mesh, in_specs=in_specs, out_specs=out_specs, check_vma=False
    )
```

```python
import functools

import jax
import jax.numpy as jnp
from jax import lax
from jax.experimental import pallas as pl
from jax.experimental.pallas import tpu as pltpu
from jax.sharding import PartitionSpec as P

BLK = 128


adapter_scale = 2.0


def row_plan(adapter_of_block, counts, adapter_slot):
    labels = jnp.arange(counts.shape[0], dtype=jnp.int32)
    matches = adapter_of_block[:, None] == labels[None, :]
    slot_of_block = jnp.sum(jnp.where(matches, adapter_slot[None, :], 0), axis=1)
    block_count = jnp.sum(jnp.where(matches, counts[None, :], 0), axis=1)
    order = jnp.arange(adapter_of_block.shape[0], dtype=jnp.int32)
    same_adapter = adapter_of_block[:, None] == adapter_of_block[None, :]
    earlier = jnp.sum(jnp.where(same_adapter & (order[None, :] < order[:, None]), 1, 0), axis=1)
    places = jnp.arange(BLK, dtype=jnp.int32)
    active_rows = jnp.where(
        earlier[:, None] * BLK + places[None, :] < block_count[:, None], 1.0, 0.0
    ).astype(jnp.float32)
    return (active_rows, slot_of_block)


def rank_terms(columns, factor_blocks, nblocks):
    pieces = columns.reshape(nblocks, BLK, columns.shape[1])
    return jnp.einsum("btc,bcr->btr", pieces, factor_blocks, preferred_element_type=jnp.float32)


def slot_total(selector, terms, slots):
    flat = terms.reshape(terms.shape[0], -1)
    summed = jnp.dot(
        selector, flat, precision=lax.Precision.HIGHEST, preferred_element_type=jnp.float32
    )
    return summed.reshape(slots, terms.shape[1], terms.shape[2]).astype(jnp.bfloat16)


def on_device(
    activations,
    cotangent,
    adapter_down_factors,
    adapter_up_factors,
    adapter_slot,
    adapter_of_block,
    counts,
):
    nblocks = adapter_of_block.shape[0]
    slots = adapter_slot.shape[0]
    active_rows, slot_of_block = row_plan(adapter_of_block, counts, adapter_slot)
    selector = (slot_of_block[None, :] == jnp.arange(slots, dtype=jnp.int32)[:, None]).astype(
        jnp.float32
    )
    down_cols, up_cols = (
        lax.all_to_all(adapter_down_factors, "rows", split_axis=1, concat_axis=0, tiled=True),
        lax.all_to_all(adapter_up_factors, "rows", split_axis=1, concat_axis=0, tiled=True),
    )
    down_factor_blocks = down_cols[slot_of_block]
    up_factor_blocks = up_cols[slot_of_block]
    input_cols, grad_cols = (
        lax.all_to_all(activations, "rows", split_axis=1, concat_axis=0, tiled=True),
        lax.all_to_all(cotangent, "rows", split_axis=1, concat_axis=0, tiled=True),
    )
    down_sum, up_partial_sum = lax.psum(
        (
            rank_terms(input_cols, down_factor_blocks, nblocks),
            rank_terms(grad_cols, up_factor_blocks, nblocks),
        ),
        ("rows", "tp"),
    )
    reduced_down = (active_rows[:, :, None] * down_sum).astype(jnp.bfloat16)
    reduced_up = (adapter_scale * active_rows[:, :, None] * up_partial_sum).astype(jnp.bfloat16)
    grad_pieces = grad_cols.reshape(nblocks, BLK, grad_cols.shape[1])
    input_pieces = input_cols.reshape(nblocks, BLK, input_cols.shape[1])
    up_contributions = adapter_scale * jnp.einsum(
        "eqi,eqf->eif", grad_pieces, reduced_down, preferred_element_type=jnp.float32
    )
    down_terms = jnp.einsum(
        "eqi,eqf->eif", input_pieces, reduced_up, preferred_element_type=jnp.float32
    )
    grad_up_cols = slot_total(selector, up_contributions, slots)
    grad_down_cols = slot_total(selector, down_terms, slots)
    input_grad_cols = jnp.einsum(
        "btr,bcr->btc", reduced_up, down_factor_blocks, preferred_element_type=jnp.float32
    )
    input_grad_cols = input_grad_cols.reshape(nblocks * BLK, input_cols.shape[1]).astype(
        jnp.bfloat16
    )
    input_grad, grad_down, grad_up = (
        lax.all_to_all(input_grad_cols, "rows", split_axis=0, concat_axis=1, tiled=True),
        lax.all_to_all(grad_down_cols, "rows", split_axis=0, concat_axis=1, tiled=True),
        lax.all_to_all(grad_up_cols, "rows", split_axis=0, concat_axis=1, tiled=True),
    )
    return (input_grad, grad_down, grad_up)


GATHER_LIMIT = 24 << 20


LANES = 2
CHUNKS = 2
MESH = pl.DeviceIdType.MESH
NT = (((1,), (1,)), ((), ()))
TN = (((0,), (0,)), ((), ()))


def line_gather(buf, piece, send, recv, rows, chunk=0, hand=True):
    line = rows // LANES
    me = lax.axis_index("rows")
    at, lane = me // LANES, me % LANES

    def copy(where, p, to):
        return pltpu.make_async_remote_copy(
            src_ref=piece(buf, p),
            dst_ref=piece(buf, p),
            send_sem=send.at[3 * chunk + where, p // LANES],
            recv_sem=recv.at[rows * chunk + p],
            device_id={"rows": to},
            device_id_type=MESH,
        )

    def arrived(p):
        copy(0, p, me ^ 1).wait_recv()

    def start():
        @pl.when(at < line - 1)
        def _():
            copy(0, me, me + LANES).start()

        @pl.when(at > 0)
        def _():
            copy(1, me, me - LANES).start()

        if hand:
            copy(2, me, me ^ 1).start()

    def forward():
        for k in range(1, line):
            low, high = me - k * LANES, me + k * LANES

            @pl.when(at - k >= 0)
            def _():
                arrived(low)

                @pl.when(at < line - 1)
                def _():
                    copy(0, low, me + LANES).start()

                if hand:
                    copy(2, low, me ^ 1).start()

            @pl.when(at + k < line)
            def _():
                arrived(high)

                @pl.when(at > 0)
                def _():
                    copy(1, high, me - LANES).start()

                if hand:
                    copy(2, high, me ^ 1).start()

    def beside():
        for z in range(line):
            arrived(z * LANES + 1 - lane)

    def drain():
        for z in range(line):
            p = z * LANES + lane
            if hand:
                copy(2, p, me ^ 1).wait_send()

            @pl.when(jnp.logical_and(z <= at, at < line - 1))
            def _():
                copy(0, p, me + LANES).wait_send()

            @pl.when(jnp.logical_and(z >= at, at > 0))
            def _():
                copy(1, p, me - LANES).wait_send()

    return start, forward, beside, drain


def tenant_kernel(
    rows,
    slot_of,
    block_adapter,
    counts,
    down_hbm,
    up_hbm,
    act_hbm,
    cot_hbm,
    input_grad,
    grad_down,
    grad_up,
    fac_low,
    fac_high,
    terms,
    totals,
    act,
    cot,
    half_out,
    half_in,
    own_half,
    beside_out,
    beside_in,
    sum_out,
    sum_in,
    wish_out,
    wish_in,
    wish,
    fac_send,
    fac_recv,
    term_send,
    term_recv,
    pair_send,
    pair_recv,
    local,
):
    me = lax.axis_index("rows")
    group = lax.axis_index("groups")
    core = lax.axis_index("tp")
    line = rows // LANES
    at, lane = me // LANES, me % LANES
    here, rank, inputs = grad_down.shape
    hidden = cot.shape[1]
    ih, hh = inputs // 2, hidden // 2
    spot = pl.ds(at * here, here)

    fac = (fac_low, fac_high)
    width = fac_low.shape[2]
    up_low, up_high = width - ih, width
    own_factors = [
        pltpu.make_async_copy(
            down_hbm.at[:, :, pl.ds(pl.multiple_of(group * ih, 128), ih)],
            fac_low.at[spot, :, pl.ds(0, ih)],
            local.at[2],
        ),
        pltpu.make_async_copy(
            up_hbm.at[:, :, pl.ds(pl.multiple_of(group * hh, 128), up_low)],
            fac_low.at[spot, :, pl.ds(ih, up_low)],
            local.at[3],
        ),
        pltpu.make_async_copy(
            up_hbm.at[:, :, pl.ds(pl.multiple_of(group * hh + up_low, 128), up_high)],
            fac_high.at[spot],
            local.at[5],
        ),
    ]
    for load in own_factors:
        load.start()
    loads = [
        pltpu.make_async_copy(act_hbm, act, local.at[0]),
        pltpu.make_async_copy(cot_hbm, cot, local.at[1]),
    ]
    for load in loads:
        load.start()

    barrier = pltpu.get_barrier_semaphore()

    def greet(target):
        pl.semaphore_signal(barrier, inc=1, device_id=target, device_id_type=MESH)

    greet({"rows": me ^ 1})
    greet({"groups": 1 - group})
    greet({"tp": 1 - core})

    @pl.when(at > 0)
    def _():
        greet({"rows": me - LANES})

    @pl.when(at < line - 1)
    def _():
        greet({"rows": me + LANES})

    adapter = block_adapter[me]
    slot = slot_of[adapter]
    earlier = jnp.int32(0)
    for b in range(rows):
        same = jnp.logical_and(block_adapter[b] == adapter, b < me)
        earlier += jnp.where(same, 1, 0)
    place = lax.broadcasted_iota(jnp.int32, (1, BLK), 1)
    live = jnp.where(earlier * BLK + place < counts[adapter], 1.0, 0.0)
    slot_beside = slot_of[block_adapter[me ^ 1]]
    row = lax.broadcasted_iota(jnp.int32, wish_out.shape, 0)
    wish_out[...] = jnp.where(row == 0, slot, slot_beside)

    for load in own_factors:
        load.wait()
    pl.semaphore_wait(
        barrier, 3 + jnp.where(at > 0, 1, 0) + jnp.where(at < line - 1, 1, 0)
    )

    def pair(source, target, which, to):
        return pltpu.make_async_remote_copy(
            src_ref=source,
            dst_ref=target,
            send_sem=pair_send.at[which],
            recv_sem=pair_recv.at[which],
            device_id=to,
            device_id_type=MESH,
        )

    chunks = [pl.ds(c * width, width) for c in range(CHUNKS)]
    gathers = [
        line_gather(
            fac[c],
            lambda r, p: r.at[pl.ds((p // LANES) * here, here)],
            fac_send,
            fac_recv,
            rows,
            chunk=c,
            hand=False,
        )
        for c in range(CHUNKS)
    ]

    def place_of(s):
        owner = s // here
        return (owner // LANES) * here + s % here, owner % LANES == lane

    ask = pair(wish_out, wish_in, 2, {"groups": 1 - group})
    hands, swaps = [], []

    def hand_over(c):
        beside_out[c, 0] = fac[c][place_of(slot_beside)[0]]
        beside_out[c, 1] = fac[c][place_of(wish[1, 0])[0]]
        hands.append(pair(beside_out.at[c], beside_in.at[c], 3 + c, {"rows": me ^ 1}))
        hands[c].start()

    def swap_over(c):
        cols = chunks[c]
        hands[c].wait_recv()
        where, local_lane = place_of(wish[0, 0])
        half_out[c] = jnp.where(local_lane, fac[c][where], beside_in[c, 1])
        swaps.append(
            pair(half_out.at[c], half_in.at[c], 3 + CHUNKS + c, {"groups": 1 - group})
        )
        swaps[c].start()
        where, local_lane = place_of(slot)
        own_half[:, cols] = jnp.where(local_lane, fac[c][where], beside_in[c, 0])

    for c in range(CHUNKS):
        start, forward, _, _ = gathers[c]
        start()
        if c == 0:
            ask.start()
        else:
            hand_over(c - 1)
        forward()
        if c == 0:
            ask.wait_recv()
            note = pltpu.make_async_copy(wish_in, wish, local.at[4])
            note.start()
            note.wait()
        else:
            swap_over(c - 1)
    hand_over(CHUNKS - 1)
    for load in loads:
        load.wait()
    swap_over(CHUNKS - 1)

    def dot(a, b, dims=(((1,), (0,)), ((), ()))):
        return lax.dot_general(a, b, dims, preferred_element_type=jnp.float32)

    def part(index, width):
        return pl.ds(pl.multiple_of(index * width, 128), width)

    own = own_half[...]
    own_down = dot(own[:, :ih], act[:, part(group, ih)], NT)
    own_up = dot(own[:, ih:], cot[:, part(group, hh)], NT)
    for swap in swaps:
        swap.wait_recv()
    other = jnp.concatenate([half_in[c] for c in range(CHUNKS)], axis=1)
    sum_out[0:rank] = own_down + dot(other[:, :ih], act[:, part(1 - group, ih)], NT)
    sum_out[rank:] = own_up + dot(other[:, ih:], cot[:, part(1 - group, hh)], NT)
    share = pair(sum_out, sum_in, 1, {"tp": 1 - core})
    share.start()
    share.wait_recv()
    sums = sum_out[...] + sum_in[...]
    low_down = (live * sums[:rank]).astype(jnp.bfloat16)
    low_up = (adapter_scale * live * sums[rank:]).astype(jnp.bfloat16)

    terms[me, :, 0:inputs] = dot(low_up, act[...]).astype(jnp.bfloat16)
    terms[me, :, inputs:] = (adapter_scale * dot(low_down, cot[...])).astype(jnp.bfloat16)
    start2, forward2, beside2, drain2 = line_gather(
        terms, lambda r, p: r.at[p], term_send, term_recv, rows
    )
    start2()
    input_grad[:, part(group, ih)] = dot(low_up, own[:, :ih], TN).astype(jnp.bfloat16)
    input_grad[:, part(1 - group, ih)] = dot(low_up, other[:, :ih], TN).astype(jnp.bfloat16)
    for gather in gathers:
        gather[3]()
    forward2()

    tile = 512

    def weights(which):
        slots = [slot_of[block_adapter[z * LANES + which]] for z in range(line)]
        return [
            [jnp.where(s == me * here + j, 1.0, 0.0) for s in slots] for j in range(here)
        ]

    def add(which, mask, source, j):
        total = mask[j][0] * terms[which, :, source].astype(jnp.float32)
        for z in range(1, line):
            total += mask[j][z] * terms[z * LANES + which, :, source].astype(jnp.float32)
        return total

    same_lane = weights(lane)

    def first(i, carry):
        source = part(i, tile)
        for j in range(here):
            totals[j, :, source] = add(lane, same_lane, source, j)
        return carry

    lax.fori_loop(0, (inputs + hidden) // tile, first, 0)
    beside2()
    other_lane = weights(1 - lane)
    for out, base, width in ((grad_down, 0, inputs), (grad_up, inputs, hidden)):

        def second(i, carry, out=out, base=base):
            source = pl.ds(pl.multiple_of(base + i * tile, tile), tile)
            for j in range(here):
                total = totals[j, :, source] + add(1 - lane, other_lane, source, j)
                out[j, :, part(i, tile)] = total.astype(jnp.bfloat16)
            return carry

        lax.fori_loop(0, width // tile, second, 0)

    drain2()
    ask.wait_send()
    for c in range(CHUNKS):
        hands[c].wait_send()
        swaps[c].wait_send()
    share.wait_send()


def tenant_plan(
    activations,
    cotangent,
    adapter_down_factors,
    adapter_up_factors,
    adapter_slot,
    adapter_of_block,
    counts,
):
    rows = jax.lax.axis_size("rows")
    here, inputs, rank = adapter_down_factors.shape
    hidden = adapter_up_factors.shape[1]
    half = (inputs + hidden) // 2
    bf16, f32, i32 = jnp.bfloat16, jnp.float32, jnp.int32
    line = rows // LANES
    vmem = pl.BlockSpec(memory_space=pltpu.VMEM)
    smem = pl.BlockSpec(memory_space=pltpu.SMEM)
    hbm = pl.BlockSpec(memory_space=pl.ANY)
    dma = pltpu.SemaphoreType.DMA
    input_grad, grad_down, grad_up = pl.pallas_call(
        functools.partial(tenant_kernel, rows),
        out_shape=(
            jax.ShapeDtypeStruct((BLK, inputs), bf16),
            jax.ShapeDtypeStruct((here, rank, inputs), bf16),
            jax.ShapeDtypeStruct((here, rank, hidden), bf16),
        ),
        in_specs=[smem, smem, smem, hbm, hbm, hbm, hbm],
        out_specs=(vmem, vmem, vmem),
        scratch_shapes=[
            pltpu.VMEM((line * here, rank, half // CHUNKS), bf16),
            pltpu.VMEM((line * here, rank, half // CHUNKS), bf16),
            pltpu.VMEM((rows, rank, inputs + hidden), bf16),
            pltpu.VMEM((here, rank, inputs + hidden), f32),
            pltpu.VMEM((BLK, inputs), bf16),
            pltpu.VMEM((BLK, hidden), bf16),
            pltpu.VMEM((CHUNKS, rank, half // CHUNKS), bf16),
            pltpu.VMEM((CHUNKS, rank, half // CHUNKS), bf16),
            pltpu.VMEM((rank, half), bf16),
            pltpu.VMEM((CHUNKS, 2, rank, half // CHUNKS), bf16),
            pltpu.VMEM((CHUNKS, 2, rank, half // CHUNKS), bf16),
            pltpu.VMEM((2 * rank, BLK), f32),
            pltpu.VMEM((2 * rank, BLK), f32),
            pltpu.VMEM((8, 128), i32),
            pltpu.VMEM((8, 128), i32),
            pltpu.SMEM((8, 128), i32),
            dma((3 * CHUNKS, line)),
            dma((rows * CHUNKS,)),
            dma((3, line)),
            dma((rows,)),
            dma((3 + 2 * CHUNKS,)),
            dma((3 + 2 * CHUNKS,)),
            dma((6,)),
        ],
        compiler_params=pltpu.CompilerParams(
            collective_id=0, has_side_effects=True, vmem_limit_bytes=40 << 20
        ),
    )(
        adapter_slot,
        adapter_of_block,
        counts,
        jnp.swapaxes(adapter_down_factors, 1, 2),
        jnp.swapaxes(adapter_up_factors, 1, 2),
        activations,
        cotangent,
    )
    return input_grad, jnp.swapaxes(grad_down, 1, 2), jnp.swapaxes(grad_up, 1, 2)


def choose(*args):
    factors = (args[2].size + args[3].size) * 2 * jax.lax.axis_size("rows")
    one_block = args[0].shape[0] == BLK
    plan = tenant_plan if one_block and jax.lax.axis_size("groups") == 2 and factors <= GATHER_LIMIT else on_device
    return plan(*args)


def solution(mesh):
    in_specs = (
        P(("groups", "rows"), "tp"),
        P(("groups", "rows"), "tp"),
        P("rows", "tp", None),
        P("rows", "tp", None),
        P(),
        P("groups"),
        P("groups"),
    )
    out_specs = (
        P(("groups", "rows"), "tp"),
        P(("groups", "rows"), "tp", None),
        P(("groups", "rows"), "tp", None),
    )
    return jax.shard_map(
        choose, mesh=mesh, in_specs=in_specs, out_specs=out_specs, check_vma=False
    )
```

```python
import functools

import jax
import jax.numpy as jnp
from jax import lax
from jax.experimental import pallas as pl
from jax.experimental.pallas import tpu as pltpu
from jax.sharding import PartitionSpec as P

BLK = 128


adapter_scale = 2.0


def row_plan(adapter_of_block, counts, adapter_slot):
    labels = jnp.arange(counts.shape[0], dtype=jnp.int32)
    matches = adapter_of_block[:, None] == labels[None, :]
    slot_of_block = jnp.sum(jnp.where(matches, adapter_slot[None, :], 0), axis=1)
    block_count = jnp.sum(jnp.where(matches, counts[None, :], 0), axis=1)
    order = jnp.arange(adapter_of_block.shape[0], dtype=jnp.int32)
    same_adapter = adapter_of_block[:, None] == adapter_of_block[None, :]
    earlier = jnp.sum(jnp.where(same_adapter & (order[None, :] < order[:, None]), 1, 0), axis=1)
    places = jnp.arange(BLK, dtype=jnp.int32)
    active_rows = jnp.where(
        earlier[:, None] * BLK + places[None, :] < block_count[:, None], 1.0, 0.0
    ).astype(jnp.float32)
    return (active_rows, slot_of_block)


def rank_terms(columns, factor_blocks, nblocks):
    pieces = columns.reshape(nblocks, BLK, columns.shape[1])
    return jnp.einsum("btc,bcr->btr", pieces, factor_blocks, preferred_element_type=jnp.float32)


def slot_total(selector, terms, slots):
    flat = terms.reshape(terms.shape[0], -1)
    summed = jnp.dot(
        selector, flat, precision=lax.Precision.HIGHEST, preferred_element_type=jnp.float32
    )
    return summed.reshape(slots, terms.shape[1], terms.shape[2]).astype(jnp.bfloat16)


def on_device(
    activations,
    cotangent,
    adapter_down_factors,
    adapter_up_factors,
    adapter_slot,
    adapter_of_block,
    counts,
):
    nblocks = adapter_of_block.shape[0]
    slots = adapter_slot.shape[0]
    active_rows, slot_of_block = row_plan(adapter_of_block, counts, adapter_slot)
    selector = (slot_of_block[None, :] == jnp.arange(slots, dtype=jnp.int32)[:, None]).astype(
        jnp.float32
    )
    down_cols, up_cols = (
        lax.all_to_all(adapter_down_factors, "rows", split_axis=1, concat_axis=0, tiled=True),
        lax.all_to_all(adapter_up_factors, "rows", split_axis=1, concat_axis=0, tiled=True),
    )
    down_factor_blocks = down_cols[slot_of_block]
    up_factor_blocks = up_cols[slot_of_block]
    input_cols, grad_cols = (
        lax.all_to_all(activations, "rows", split_axis=1, concat_axis=0, tiled=True),
        lax.all_to_all(cotangent, "rows", split_axis=1, concat_axis=0, tiled=True),
    )
    down_sum, up_partial_sum = lax.psum(
        (
            rank_terms(input_cols, down_factor_blocks, nblocks),
            rank_terms(grad_cols, up_factor_blocks, nblocks),
        ),
        ("rows", "tp"),
    )
    reduced_down = (active_rows[:, :, None] * down_sum).astype(jnp.bfloat16)
    reduced_up = (adapter_scale * active_rows[:, :, None] * up_partial_sum).astype(jnp.bfloat16)
    grad_pieces = grad_cols.reshape(nblocks, BLK, grad_cols.shape[1])
    input_pieces = input_cols.reshape(nblocks, BLK, input_cols.shape[1])
    up_contributions = adapter_scale * jnp.einsum(
        "eqi,eqf->eif", grad_pieces, reduced_down, preferred_element_type=jnp.float32
    )
    down_terms = jnp.einsum(
        "eqi,eqf->eif", input_pieces, reduced_up, preferred_element_type=jnp.float32
    )
    grad_up_cols = slot_total(selector, up_contributions, slots)
    grad_down_cols = slot_total(selector, down_terms, slots)
    input_grad_cols = jnp.einsum(
        "btr,bcr->btc", reduced_up, down_factor_blocks, preferred_element_type=jnp.float32
    )
    input_grad_cols = input_grad_cols.reshape(nblocks * BLK, input_cols.shape[1]).astype(
        jnp.bfloat16
    )
    input_grad, grad_down, grad_up = (
        lax.all_to_all(input_grad_cols, "rows", split_axis=0, concat_axis=1, tiled=True),
        lax.all_to_all(grad_down_cols, "rows", split_axis=0, concat_axis=1, tiled=True),
        lax.all_to_all(grad_up_cols, "rows", split_axis=0, concat_axis=1, tiled=True),
    )
    return (input_grad, grad_down, grad_up)


GATHER_LIMIT = 24 << 20


LANES = 2
MESH = pl.DeviceIdType.MESH
NT = (((1,), (1,)), ((), ()))
TN = (((0,), (0,)), ((), ()))


def line_gather(buf, piece, send, recv, rows):
    line = rows // LANES
    me = lax.axis_index("rows")
    at, lane = me // LANES, me % LANES

    def copy(where, p, to):
        return pltpu.make_async_remote_copy(
            src_ref=piece(buf, p),
            dst_ref=piece(buf, p),
            send_sem=send.at[where, p // LANES],
            recv_sem=recv.at[p],
            device_id={"rows": to},
            device_id_type=MESH,
        )

    def arrived(p):
        copy(0, p, me ^ 1).wait_recv()

    def start():
        @pl.when(at < line - 1)
        def _():
            copy(0, me, me + LANES).start()

        @pl.when(at > 0)
        def _():
            copy(1, me, me - LANES).start()

        copy(2, me, me ^ 1).start()

    def forward():
        for k in range(1, line):
            low, high = me - k * LANES, me + k * LANES

            @pl.when(at - k >= 0)
            def _():
                arrived(low)

                @pl.when(at < line - 1)
                def _():
                    copy(0, low, me + LANES).start()

                copy(2, low, me ^ 1).start()

            @pl.when(at + k < line)
            def _():
                arrived(high)

                @pl.when(at > 0)
                def _():
                    copy(1, high, me - LANES).start()

                copy(2, high, me ^ 1).start()

    def beside():
        for z in range(line):
            arrived(z * LANES + 1 - lane)

    def drain():
        for z in range(line):
            p = z * LANES + lane
            copy(2, p, me ^ 1).wait_send()

            @pl.when(jnp.logical_and(z <= at, at < line - 1))
            def _():
                copy(0, p, me + LANES).wait_send()

            @pl.when(jnp.logical_and(z >= at, at > 0))
            def _():
                copy(1, p, me - LANES).wait_send()

    return start, forward, beside, drain


def tenant_kernel(
    rows,
    slot_of,
    block_adapter,
    counts,
    down_hbm,
    up_hbm,
    act_hbm,
    cot_hbm,
    input_grad,
    grad_down,
    grad_up,
    fac,
    terms,
    totals,
    act,
    cot,
    half_out,
    half_in,
    sum_out,
    sum_in,
    wish_out,
    wish_in,
    wish,
    fac_send,
    fac_recv,
    term_send,
    term_recv,
    pair_send,
    pair_recv,
    local,
):
    me = lax.axis_index("rows")
    group = lax.axis_index("groups")
    core = lax.axis_index("tp")
    line = rows // LANES
    at, lane = me // LANES, me % LANES
    here, rank, inputs = grad_down.shape
    hidden = cot.shape[1]
    ih, hh = inputs // 2, hidden // 2
    spot = pl.ds(me * here, here)

    own_factors = [
        pltpu.make_async_copy(
            down_hbm.at[:, :, pl.ds(pl.multiple_of(group * ih, 128), ih)],
            fac.at[spot, :, pl.ds(0, ih)],
            local.at[2],
        ),
        pltpu.make_async_copy(
            up_hbm.at[:, :, pl.ds(pl.multiple_of(group * hh, 128), hh)],
            fac.at[spot, :, pl.ds(ih, hh)],
            local.at[3],
        ),
    ]
    for load in own_factors:
        load.start()
    loads = [
        pltpu.make_async_copy(act_hbm, act, local.at[0]),
        pltpu.make_async_copy(cot_hbm, cot, local.at[1]),
    ]
    for load in loads:
        load.start()

    barrier = pltpu.get_barrier_semaphore()

    def greet(target):
        pl.semaphore_signal(barrier, inc=1, device_id=target, device_id_type=MESH)

    greet({"rows": me ^ 1})
    greet({"groups": 1 - group})
    greet({"tp": 1 - core})

    @pl.when(at > 0)
    def _():
        greet({"rows": me - LANES})

    @pl.when(at < line - 1)
    def _():
        greet({"rows": me + LANES})

    adapter = block_adapter[me]
    slot = slot_of[adapter]
    earlier = jnp.int32(0)
    for b in range(rows):
        same = jnp.logical_and(block_adapter[b] == adapter, b < me)
        earlier += jnp.where(same, 1, 0)
    place = lax.broadcasted_iota(jnp.int32, (1, BLK), 1)
    live = jnp.where(earlier * BLK + place < counts[adapter], 1.0, 0.0)
    wish_out[...] = jnp.full(wish_out.shape, slot, jnp.int32)

    for load in own_factors:
        load.wait()
    pl.semaphore_wait(
        barrier, 3 + jnp.where(at > 0, 1, 0) + jnp.where(at < line - 1, 1, 0)
    )

    def pair(source, target, which, to):
        return pltpu.make_async_remote_copy(
            src_ref=source,
            dst_ref=target,
            send_sem=pair_send.at[which],
            recv_sem=pair_recv.at[which],
            device_id=to,
            device_id_type=MESH,
        )

    start, forward, beside, drain = line_gather(
        fac, lambda r, p: r.at[pl.ds(p * here, here)], fac_send, fac_recv, rows
    )
    start()
    ask = pair(wish_out, wish_in, 2, {"groups": 1 - group})
    ask.start()
    forward()
    ask.wait_recv()
    note = pltpu.make_async_copy(wish_in, wish, local.at[4])
    note.start()
    note.wait()
    for load in loads:
        load.wait()
    beside()

    half_out[...] = fac[wish[0, 0]]
    swap = pair(half_out, half_in, 0, {"groups": 1 - group})
    swap.start()

    def dot(a, b, dims=(((1,), (0,)), ((), ()))):
        return lax.dot_general(a, b, dims, preferred_element_type=jnp.float32)

    def part(index, width):
        return pl.ds(pl.multiple_of(index * width, 128), width)

    own = fac[slot]
    own_down = dot(own[:, :ih], act[:, part(group, ih)], NT)
    own_up = dot(own[:, ih:], cot[:, part(group, hh)], NT)
    swap.wait_recv()
    other = half_in[...]
    sum_out[0:rank] = own_down + dot(other[:, :ih], act[:, part(1 - group, ih)], NT)
    sum_out[rank:] = own_up + dot(other[:, ih:], cot[:, part(1 - group, hh)], NT)
    share = pair(sum_out, sum_in, 1, {"tp": 1 - core})
    share.start()
    share.wait_recv()
    sums = sum_out[...] + sum_in[...]
    low_down = (live * sums[:rank]).astype(jnp.bfloat16)
    low_up = (adapter_scale * live * sums[rank:]).astype(jnp.bfloat16)

    terms[me, :, 0:inputs] = dot(low_up, act[...]).astype(jnp.bfloat16)
    terms[me, :, inputs:] = (adapter_scale * dot(low_down, cot[...])).astype(jnp.bfloat16)
    start2, forward2, beside2, drain2 = line_gather(
        terms, lambda r, p: r.at[p], term_send, term_recv, rows
    )
    start2()
    input_grad[:, part(group, ih)] = dot(low_up, own[:, :ih], TN).astype(jnp.bfloat16)
    input_grad[:, part(1 - group, ih)] = dot(low_up, other[:, :ih], TN).astype(jnp.bfloat16)
    drain()
    forward2()

    tile = 512

    def weights(which):
        slots = [slot_of[block_adapter[z * LANES + which]] for z in range(line)]
        return [
            [jnp.where(s == me * here + j, 1.0, 0.0) for s in slots] for j in range(here)
        ]

    def add(which, mask, source, j):
        total = mask[j][0] * terms[which, :, source].astype(jnp.float32)
        for z in range(1, line):
            total += mask[j][z] * terms[z * LANES + which, :, source].astype(jnp.float32)
        return total

    same_lane = weights(lane)

    def first(i, carry):
        source = part(i, tile)
        for j in range(here):
            totals[j, :, source] = add(lane, same_lane, source, j)
        return carry

    lax.fori_loop(0, (inputs + hidden) // tile, first, 0)
    beside2()
    other_lane = weights(1 - lane)
    for out, base, width in ((grad_down, 0, inputs), (grad_up, inputs, hidden)):

        def second(i, carry, out=out, base=base):
            source = pl.ds(pl.multiple_of(base + i * tile, tile), tile)
            for j in range(here):
                total = totals[j, :, source] + add(1 - lane, other_lane, source, j)
                out[j, :, part(i, tile)] = total.astype(jnp.bfloat16)
            return carry

        lax.fori_loop(0, width // tile, second, 0)

    drain2()
    ask.wait_send()
    swap.wait_send()
    share.wait_send()


def tenant_plan(
    activations,
    cotangent,
    adapter_down_factors,
    adapter_up_factors,
    adapter_slot,
    adapter_of_block,
    counts,
):
    rows = jax.lax.axis_size("rows")
    here, inputs, rank = adapter_down_factors.shape
    hidden = adapter_up_factors.shape[1]
    half = (inputs + hidden) // 2
    bf16, f32, i32 = jnp.bfloat16, jnp.float32, jnp.int32
    line = rows // LANES
    vmem = pl.BlockSpec(memory_space=pltpu.VMEM)
    smem = pl.BlockSpec(memory_space=pltpu.SMEM)
    hbm = pl.BlockSpec(memory_space=pl.ANY)
    dma = pltpu.SemaphoreType.DMA
    input_grad, grad_down, grad_up = pl.pallas_call(
        functools.partial(tenant_kernel, rows),
        out_shape=(
            jax.ShapeDtypeStruct((BLK, inputs), bf16),
            jax.ShapeDtypeStruct((here, rank, inputs), bf16),
            jax.ShapeDtypeStruct((here, rank, hidden), bf16),
        ),
        in_specs=[smem, smem, smem, hbm, hbm, hbm, hbm],
        out_specs=(vmem, vmem, vmem),
        scratch_shapes=[
            pltpu.VMEM((rows * here, rank, half), bf16),
            pltpu.VMEM((rows, rank, inputs + hidden), bf16),
            pltpu.VMEM((here, rank, inputs + hidden), f32),
            pltpu.VMEM((BLK, inputs), bf16),
            pltpu.VMEM((BLK, hidden), bf16),
            pltpu.VMEM((rank, half), bf16),
            pltpu.VMEM((rank, half), bf16),
            pltpu.VMEM((2 * rank, BLK), f32),
            pltpu.VMEM((2 * rank, BLK), f32),
            pltpu.VMEM((8, 128), i32),
            pltpu.VMEM((8, 128), i32),
            pltpu.SMEM((8, 128), i32),
            dma((3, line)),
            dma((rows,)),
            dma((3, line)),
            dma((rows,)),
            dma((3,)),
            dma((3,)),
            dma((5,)),
        ],
        compiler_params=pltpu.CompilerParams(
            collective_id=0, has_side_effects=True, vmem_limit_bytes=60 << 20
        ),
    )(
        adapter_slot,
        adapter_of_block,
        counts,
        jnp.swapaxes(adapter_down_factors, 1, 2),
        jnp.swapaxes(adapter_up_factors, 1, 2),
        activations,
        cotangent,
    )
    return input_grad, jnp.swapaxes(grad_down, 1, 2), jnp.swapaxes(grad_up, 1, 2)


def choose(*args):
    factors = (args[2].size + args[3].size) * 2 * jax.lax.axis_size("rows")
    one_block = args[0].shape[0] == BLK
    plan = tenant_plan if one_block and jax.lax.axis_size("groups") == 2 and factors <= GATHER_LIMIT else on_device
    return plan(*args)


def solution(mesh):
    in_specs = (
        P(("groups", "rows"), "tp"),
        P(("groups", "rows"), "tp"),
        P("rows", "tp", None),
        P("rows", "tp", None),
        P(),
        P("groups"),
        P("groups"),
    )
    out_specs = (
        P(("groups", "rows"), "tp"),
        P(("groups", "rows"), "tp", None),
        P(("groups", "rows"), "tp", None),
    )
    return jax.shard_map(
        choose, mesh=mesh, in_specs=in_specs, out_specs=out_specs, check_vma=False
    )
```
